32 devices in a mesh: mom: 4 (over y, x), trow: 4 (over z), tcol: 2 (over core).
Axes of the slice: x: 2, y: 2, z: 4, core: 2. Of those that a mesh axis runs over, the one named last changes fastest.
Arguments:
- g_free: float32 [2, 4, 1536, 1536], P(None, 'mom', 'tcol', 'trow'), may hold values from -6 to 6
- g_greater_t: float32 [2, 4, 1536, 1536], P(None, 'mom', 'tcol', 'trow'), may hold values from -6 to 6
- momentum_map: int32 [4], replicated, may hold values from 0 to 3, each once
- weights: float32 [1536], replicated, may hold values from 0.00076546555 to 0.0076546553
Outputs:
- g_out: float32 [2, 4, 1536, 1536], P(None, 'mom', 'tcol', 'trow')
The draws below stay inside these ranges and needn't reach their ends.
Inputs may be any that keep to these rules, and one draw needn't show every extreme that they name: `momentum_map`: each number appears once.
All inputs are finite; a program needn't handle non-finite values.
Results may differ from the reference program's by a relative error of at most 0.00022.
Values sent between devices are 32-bit elements; how exact they have to be, the bound alone decides.
A program may use at most 128 MiB of HBM per device.

```python
import math
import jax
import jax.numpy as jnp
from jax import lax

LY = 4
K = 4
NT = 1536
ITERS = 2


def block_levels(rng, dims, cuts, smallest, high):
    gain = 1.0
    for dim, parts in cuts:
        draws = jax.random.uniform(jax.random.fold_in(jax.random.fold_in(rng, 6), dim), (parts,), jnp.float32, smallest / len(cuts), high / len(cuts))
        gain = gain * jnp.repeat(jnp.exp(draws), dims[dim] // parts).reshape((-1,) + (1,) * (len(dims) - 1 - dim))
    return gain


def scatter_about(stream_key, dims, width, most, cuts=(), held_as=jnp.bfloat16):
    level = block_levels(stream_key, dims, cuts, -0.22, 0.18) if cuts else 1.0
    values = jax.random.normal(stream_key, dims, jnp.float32) * width * level
    return jnp.minimum(jnp.maximum(values, -most), most).astype(held_as)


def setup_inputs(seed: int = 0) -> dict:
    streams_of = jax.random.split(jax.random.key(seed), 5)
    g_free = scatter_about(streams_of[0], (2, K, NT, NT), 1.0, 6.0, ((1, 4), (2, 2), (3, 4)), jnp.float32)
    g_greater_t = scatter_about(streams_of[1], (2, K, NT, NT), 1.0, 6.0, ((1, 4), (2, 2), (3, 4)), jnp.float32)
    momentum_map = jax.random.permutation(streams_of[2], K).astype(jnp.int32)
    weights = jnp.clip(jnp.exp(jax.random.uniform(streams_of[3], (NT,), jnp.float32, math.log(0.00076546555), math.log(0.0076546553))), 0.00076546555, 0.0076546553)
    return dict(g_free=g_free, g_greater_t=g_greater_t, momentum_map=momentum_map, weights=weights)


highest = lax.Precision.HIGHEST

def matmul(left_side, right_side):
    return jnp.dot(left_side, right_side, precision=highest, preferred_element_type=jnp.float32)

def phase_tables(momentum_map):
    momenta = momentum_map.shape[0]
    across = momenta // LY
    site_index = jnp.arange(momenta, dtype=jnp.int32)
    wave_x = momentum_map % across
    wave_y = momentum_map // across
    site_x = site_index % across
    site_y = site_index // across
    phase_turns = site_x[:, None] * wave_x[None, :] % across * LY + site_y[:, None] * wave_y[None, :] % LY * across
    angles = phase_turns.astype(jnp.float32) * (2.0 * math.pi / momenta)
    norm_scale = 1.0 / math.sqrt(momenta)
    return (jnp.cos(angles) * norm_scale, jnp.sin(angles) * norm_scale)

def mirrored(cosine_table, sine_table, real_part, imag_part):
    return (matmul(cosine_table, real_part) + matmul(sine_table, imag_part), matmul(cosine_table, imag_part) - matmul(sine_table, real_part))

def self_energy(cosine_table, sine_table, lesser_real, lesser_imag, mirror_real, mirror_imag):
    space_real = matmul(cosine_table, lesser_real) - matmul(sine_table, lesser_imag)
    space_imag = matmul(sine_table, lesser_real) + matmul(cosine_table, lesser_imag)
    square_real = space_real * space_real - space_imag * space_imag
    square_imag = 2.0 * space_real * space_imag
    source_real = square_real * mirror_real - square_imag * mirror_imag
    source_imag = square_real * mirror_imag + square_imag * mirror_real
    sigma_real = matmul(cosine_table.T, source_real) + matmul(sine_table.T, source_imag)
    sigma_imag = matmul(cosine_table.T, source_imag) - matmul(sine_table.T, source_real)
    return jnp.stack([sigma_real, sigma_imag])

def contract(left_side, right_side):
    return jnp.einsum('krs,ksc->krc', left_side, right_side, precision=highest, preferred_element_type=jnp.float32)

def weighted_product(sigma_part, green_part):
    real_part = contract(sigma_part[0], green_part[0]) - contract(sigma_part[1], green_part[1])
    imag_part = contract(sigma_part[0], green_part[1]) + contract(sigma_part[1], green_part[0])
    return jnp.stack([real_part, imag_part])

def reference(g_free, g_greater_t, momentum_map, weights):
    cosine_table, sine_table = phase_tables(momentum_map)
    cells = NT * NT
    greater_flat = g_greater_t.reshape(2, K, cells)
    mirror_real, mirror_imag = mirrored(cosine_table, sine_table, greater_flat[0], greater_flat[1])
    green_now = g_free
    for sweep in range(ITERS):
        flat = green_now.reshape(2, K, cells)
        sigma_full = self_energy(cosine_table, sine_table, flat[0], flat[1], mirror_real, mirror_imag).reshape(2, K, NT, NT)
        sigma_weighted = sigma_full * weights

        def one_momentum(pair):
            return weighted_product(pair[0][:, None], pair[1][:, None])[:, 0]
        correction = lax.map(one_momentum, (jnp.moveaxis(sigma_weighted, 1, 0), jnp.moveaxis(green_now, 1, 0)))
        green_now = g_free + jnp.moveaxis(correction, 0, 1)
    return green_now
```

```python
import functools
import math

import jax
import jax.numpy as jnp
from jax import lax
from jax.experimental import pallas as pl
from jax.experimental.pallas import tpu as pltpu
from jax.sharding import PartitionSpec as P

LY = 4
ITERS = 2
CHUNKS = 4
SUBLANES = 8


def phase_tables(momentum_map):
    momenta = momentum_map.shape[0]
    across = momenta // LY
    site_index = jnp.arange(momenta, dtype=jnp.int32)
    wave_x = momentum_map % across
    wave_y = momentum_map // across
    site_x = site_index % across
    site_y = site_index // across
    phase_turns = (
        site_x[:, None] * wave_x[None, :] % across * LY
        + site_y[:, None] * wave_y[None, :] % LY * across
    )
    angles = phase_turns.astype(jnp.float32) * (2.0 * math.pi / momenta)
    norm_scale = 1.0 / math.sqrt(momenta)
    return (jnp.cos(angles) * norm_scale, jnp.sin(angles) * norm_scale)


def over_sites(momenta, one_site):
    if momenta <= 8:
        for site in range(momenta):
            one_site(site, site == 0)
    else:
        one_site(0, True)
        pl.loop(1, momenta)(lambda site: one_site(site, False))


def transform(cos_ref, sin_ref, site, reals, imags, sign):
    total_real = total_imag = None
    for k, (real, imag) in enumerate(zip(reals, imags)):
        c = cos_ref[site, k]
        s = sin_ref[site, k]
        if sign < 0:
            term_real, term_imag = c * real + s * imag, c * imag - s * real
        else:
            term_real, term_imag = c * real - s * imag, c * imag + s * real
        total_real = term_real if k == 0 else total_real + term_real
        total_imag = term_imag if k == 0 else total_imag + term_imag
    return total_real, total_imag


def momentum_values(refs, local_mom, rows):
    reals = [ref[0, j, rows, :] for ref in refs for j in range(local_mom)]
    imags = [ref[1, j, rows, :] for ref in refs for j in range(local_mom)]
    return reals, imags


def mirror_kernel(groups, local_mom, *refs):
    cos_ref, sin_ref = refs[:2]
    ins = refs[2 : 2 + groups]
    out = refs[2 + groups]
    height = out.shape[2]

    @pl.loop(0, height // SUBLANES)
    def _(step):
        rows = pl.ds(pl.multiple_of(step * SUBLANES, SUBLANES), SUBLANES)
        reals, imags = momentum_values(ins, local_mom, rows)

        def one_site(site, first):
            real, imag = transform(cos_ref, sin_ref, site, reals, imags, -1)
            out[0, site, rows, :] = real
            out[1, site, rows, :] = imag

        over_sites(groups * local_mom, one_site)


def sigma_kernel(groups, local_mom, *refs):
    cos_ref, sin_ref = refs[:2]
    ins = refs[2 : 2 + groups]
    mirror = refs[2 + groups]
    outs = refs[3 + groups :]
    height = mirror.shape[2]
    momenta = groups * local_mom

    @pl.loop(0, height // SUBLANES)
    def _(step):
        rows = pl.ds(pl.multiple_of(step * SUBLANES, SUBLANES), SUBLANES)
        reals, imags = momentum_values(ins, local_mom, rows)
        held = {}

        def one_site(site, first):
            a, b = transform(cos_ref, sin_ref, site, reals, imags, 1)
            square_real = a * a - b * b
            square_imag = 2.0 * a * b
            m_real = mirror[0, site, rows, :]
            m_imag = mirror[1, site, rows, :]
            source_real = square_real * m_real - square_imag * m_imag
            source_imag = square_real * m_imag + square_imag * m_real
            for k in range(momenta):
                c = cos_ref[site, k]
                s = sin_ref[site, k]
                term = (c * source_real + s * source_imag, c * source_imag - s * source_real)
                if momenta <= 8:
                    held[k] = term if first else (held[k][0] + term[0], held[k][1] + term[1])
                else:
                    ref, j = outs[k // local_mom], k % local_mom
                    for part in range(2):
                        before = 0.0 if first else ref[part, j, rows, :]
                        ref[part, j, rows, :] = before + term[part]

        over_sites(momenta, one_site)
        for k, term in held.items():
            ref, j = outs[k // local_mom], k % local_mom
            ref[0, j, rows, :] = term[0]
            ref[1, j, rows, :] = term[1]


def call_local(kernel, tables, operands, shapes):
    smem = pl.BlockSpec(memory_space=pltpu.SMEM)
    vmem = pl.BlockSpec(memory_space=pltpu.VMEM)
    cells = math.prod(operands[0].shape) * len(operands)
    return pl.pallas_call(
        kernel,
        out_shape=[jax.ShapeDtypeStruct(s, jnp.float32) for s in shapes],
        in_specs=[smem, smem] + [vmem] * len(operands),
        out_specs=[vmem] * len(shapes),
        compiler_params=pltpu.CompilerParams(vmem_limit_bytes=32 * 2**20),
        cost_estimate=pl.CostEstimate(flops=40 * cells, bytes_accessed=12 * cells, transcendentals=0),
    )(*tables, *operands)


def body(g_free, g_greater_t, momentum_map, weights):
    cosine_table, sine_table = phase_tables(momentum_map)
    groups = lax.axis_size("mom")
    me = lax.axis_index("mom")
    line = lax.axis_size("trow")
    place = lax.axis_index("trow")
    _, local_mom, tile_rows, tile_cols = g_free.shape
    momenta = groups * local_mom
    half = line // 2
    chunks = CHUNKS
    while tile_rows % (chunks * groups * SUBLANES):
        chunks -= 1
    piece_rows = tile_rows // (chunks * groups)
    chunk_rows = piece_rows * groups
    part_cols = half * tile_cols

    def rolled(rows_first, start):
        shape = rows_first.shape
        cut = rows_first.reshape((chunks, groups, piece_rows) + shape[1:])
        twice = jnp.concatenate([cut, cut], axis=1)
        return lax.dynamic_slice_in_dim(twice, start, groups, 1).reshape(shape)

    def rotate(tile, axis):
        return jnp.moveaxis(rolled(jnp.moveaxis(tile, axis, 0), me), 0, axis)

    def unrotate(tile, axis):
        back = lax.rem(groups - me, groups)
        return jnp.moveaxis(rolled(jnp.moveaxis(tile, axis, 0), back), 0, axis)

    order = (me - jnp.arange(groups, dtype=jnp.int32)) % groups
    columns = (order[:, None] * local_mom + jnp.arange(local_mom, dtype=jnp.int32)).reshape(-1)
    tables = (jnp.take(cosine_table, columns, axis=1), jnp.take(sine_table, columns, axis=1))

    def shifted(value, by):
        if by % groups == 0:
            return value
        return lax.ppermute(value, "mom", [(i, (i + by) % groups) for i in range(groups)])

    def to_sites(chunk):
        return [
            shifted(chunk[:, :, s * piece_rows : (s + 1) * piece_rows], s) for s in range(groups)
        ]

    def to_momentum(pieces):
        return jnp.concatenate([shifted(p, -s) for s, p in enumerate(pieces)], axis=2)

    inward = [(j, j + 1) for j in range(half - 1)] + [(j, j - 1) for j in range(half + 1, line)]
    across = [(half - 1, half), (half, half - 1)]
    low = place < half
    distance = jnp.where(low, half - 1 - place, place - half)

    def near_tiles(tile):
        tiles = [tile]
        for _ in range(half - 1):
            tiles.append(lax.ppermute(tiles[-1], "trow", inward))
        return tiles

    def all_times(sigma):
        near = near_tiles(sigma)
        far = [lax.ppermute(t, "trow", across) for t in near]
        blocks = [jnp.where(low, a, b) for a, b in zip(near[::-1] + far, far[::-1] + near)]
        joined = jnp.concatenate(blocks, axis=3) * weights
        return jnp.concatenate([joined[0], joined[1]], axis=1)

    def outward(tiles):
        result = tiles[0]
        for d in range(1, half):
            moving = tiles[d]
            for step in range(1, d + 1):
                pairs = [(half - step, half - 1 - step), (half - 1 + step, half + step)]
                moving = lax.ppermute(moving, "trow", pairs)
            result = jnp.where(distance == d, moving, result)
        return result

    free = rotate(g_free, 2)
    greater = rotate(g_greater_t, 2)

    def chunk_of(tile, axis, c):
        return lax.slice_in_dim(tile, c * chunk_rows, (c + 1) * chunk_rows, axis=axis)

    piece = (2, local_mom, piece_rows, tile_cols)
    greens = [chunk_of(free, 2, c) for c in range(chunks)]
    near_free = near_tiles(g_free)
    hub_plain = jnp.concatenate([t[0] for t in near_free] + [t[1] for t in near_free], axis=2)
    hub_free = rotate(hub_plain, 1)
    right_side = lax.all_gather(hub_plain, "tcol", axis=1, tiled=True)
    mirrors = []
    for sweep in range(ITERS):
        hub_chunks, next_greens = [], []
        for c in range(chunks):
            lesser = to_sites(greens[c])
            if sweep == 0:
                mirrors.append(
                    call_local(
                        functools.partial(mirror_kernel, groups, local_mom),
                        tables,
                        to_sites(chunk_of(greater, 2, c)),
                        [(2, momenta, piece_rows, tile_cols)],
                    )[0]
                )
            sigma = to_momentum(
                call_local(
                    functools.partial(sigma_kernel, groups, local_mom),
                    tables,
                    lesser + [mirrors[c]],
                    [piece] * groups,
                )
            )
            left_side = all_times(sigma)
            product = jnp.einsum(
                "krs,ksc->krc",
                left_side,
                right_side,
                precision=lax.Precision.HIGH,
                preferred_element_type=jnp.float32,
            )
            top, bottom = product[:, :chunk_rows], product[:, chunk_rows:]
            real = top[:, :, :part_cols] - bottom[:, :, part_cols:]
            imag = top[:, :, part_cols:] + bottom[:, :, :part_cols]
            hub = chunk_of(hub_free, 1, c) + jnp.concatenate([real, imag], axis=2)
            hub_chunks.append(hub)
            tiles = [
                jnp.stack(
                    [
                        lax.slice_in_dim(hub, col, col + tile_cols, axis=2)
                        for col in (d * tile_cols, part_cols + d * tile_cols)
                    ]
                )
                for d in range(half)
            ]
            next_greens.append(outward(tiles))
        greens = next_greens
        if sweep < ITERS - 1:
            whole = unrotate(jnp.concatenate(hub_chunks, axis=1), 1)
            right_side = lax.all_gather(whole, "tcol", axis=1, tiled=True)
    return unrotate(jnp.concatenate(greens, axis=2), 2)


def solution(mesh):
    placed = (P(None, "mom", "tcol", "trow"), P(None, "mom", "tcol", "trow"), P(), P())
    return jax.shard_map(
        body, mesh=mesh, in_specs=placed, out_specs=P(None, "mom", "tcol", "trow"), check_vma=False
    )
```

```python
import functools
import math

import jax
import jax.numpy as jnp
from jax import lax
from jax.experimental import pallas as pl
from jax.experimental.pallas import tpu as pltpu
from jax.sharding import PartitionSpec as P

LY = 4
ITERS = 2
CHUNKS = 4
SUBLANES = 8


def phase_tables(momentum_map):
    momenta = momentum_map.shape[0]
    across = momenta // LY
    site_index = jnp.arange(momenta, dtype=jnp.int32)
    wave_x = momentum_map % across
    wave_y = momentum_map // across
    site_x = site_index % across
    site_y = site_index // across
    phase_turns = (
        site_x[:, None] * wave_x[None, :] % across * LY
        + site_y[:, None] * wave_y[None, :] % LY * across
    )
    angles = phase_turns.astype(jnp.float32) * (2.0 * math.pi / momenta)
    norm_scale = 1.0 / math.sqrt(momenta)
    return (jnp.cos(angles) * norm_scale, jnp.sin(angles) * norm_scale)


def over_sites(momenta, one_site):
    if momenta <= 8:
        for site in range(momenta):
            one_site(site, site == 0)
    else:
        one_site(0, True)
        pl.loop(1, momenta)(lambda site: one_site(site, False))


def transform(cos_ref, sin_ref, site, reals, imags, sign):
    total_real = total_imag = None
    for k, (real, imag) in enumerate(zip(reals, imags)):
        c = cos_ref[site, k]
        s = sin_ref[site, k]
        if sign < 0:
            term_real, term_imag = c * real + s * imag, c * imag - s * real
        else:
            term_real, term_imag = c * real - s * imag, c * imag + s * real
        total_real = term_real if k == 0 else total_real + term_real
        total_imag = term_imag if k == 0 else total_imag + term_imag
    return total_real, total_imag


def momentum_values(refs, local_mom, rows):
    reals = [ref[0, j, rows, :] for ref in refs for j in range(local_mom)]
    imags = [ref[1, j, rows, :] for ref in refs for j in range(local_mom)]
    return reals, imags


def mirror_kernel(groups, local_mom, *refs):
    cos_ref, sin_ref = refs[:2]
    ins = refs[2 : 2 + groups]
    out = refs[2 + groups]
    height = out.shape[2]

    @pl.loop(0, height // SUBLANES)
    def _(step):
        rows = pl.ds(pl.multiple_of(step * SUBLANES, SUBLANES), SUBLANES)
        reals, imags = momentum_values(ins, local_mom, rows)

        def one_site(site, first):
            real, imag = transform(cos_ref, sin_ref, site, reals, imags, -1)
            out[0, site, rows, :] = real
            out[1, site, rows, :] = imag

        over_sites(groups * local_mom, one_site)


def sigma_kernel(groups, local_mom, *refs):
    cos_ref, sin_ref = refs[:2]
    ins = refs[2 : 2 + groups]
    mirror = refs[2 + groups]
    outs = refs[3 + groups :]
    height = mirror.shape[2]
    momenta = groups * local_mom

    @pl.loop(0, height // SUBLANES)
    def _(step):
        rows = pl.ds(pl.multiple_of(step * SUBLANES, SUBLANES), SUBLANES)
        reals, imags = momentum_values(ins, local_mom, rows)
        held = {}

        def one_site(site, first):
            a, b = transform(cos_ref, sin_ref, site, reals, imags, 1)
            square_real = a * a - b * b
            square_imag = 2.0 * a * b
            m_real = mirror[0, site, rows, :]
            m_imag = mirror[1, site, rows, :]
            source_real = square_real * m_real - square_imag * m_imag
            source_imag = square_real * m_imag + square_imag * m_real
            for k in range(momenta):
                c = cos_ref[site, k]
                s = sin_ref[site, k]
                term = (c * source_real + s * source_imag, c * source_imag - s * source_real)
                if momenta <= 8:
                    held[k] = term if first else (held[k][0] + term[0], held[k][1] + term[1])
                else:
                    ref, j = outs[k // local_mom], k % local_mom
                    for part in range(2):
                        before = 0.0 if first else ref[part, j, rows, :]
                        ref[part, j, rows, :] = before + term[part]

        over_sites(momenta, one_site)
        for k, term in held.items():
            ref, j = outs[k // local_mom], k % local_mom
            ref[0, j, rows, :] = term[0]
            ref[1, j, rows, :] = term[1]


def call_local(kernel, tables, operands, shapes):
    smem = pl.BlockSpec(memory_space=pltpu.SMEM)
    vmem = pl.BlockSpec(memory_space=pltpu.VMEM)
    cells = math.prod(operands[0].shape) * len(operands)
    return pl.pallas_call(
        kernel,
        out_shape=[jax.ShapeDtypeStruct(s, jnp.float32) for s in shapes],
        in_specs=[smem, smem] + [vmem] * len(operands),
        out_specs=[vmem] * len(shapes),
        compiler_params=pltpu.CompilerParams(vmem_limit_bytes=32 * 2**20),
        cost_estimate=pl.CostEstimate(flops=40 * cells, bytes_accessed=12 * cells, transcendentals=0),
    )(*tables, *operands)


def body(g_free, g_greater_t, momentum_map, weights):
    cosine_table, sine_table = phase_tables(momentum_map)
    groups = lax.axis_size("mom")
    me = lax.axis_index("mom")
    line = lax.axis_size("trow")
    place = lax.axis_index("trow")
    _, local_mom, tile_rows, tile_cols = g_free.shape
    momenta = groups * local_mom
    half = line // 2
    chunks = CHUNKS
    while tile_rows % (chunks * groups * SUBLANES):
        chunks -= 1
    piece_rows = tile_rows // (chunks * groups)
    chunk_rows = piece_rows * groups
    part_cols = half * tile_cols

    def rolled(rows_first, start):
        shape = rows_first.shape
        cut = rows_first.reshape((chunks, groups, piece_rows) + shape[1:])
        twice = jnp.concatenate([cut, cut], axis=1)
        return lax.dynamic_slice_in_dim(twice, start, groups, 1).reshape(shape)

    def rotate(tile, axis):
        return jnp.moveaxis(rolled(jnp.moveaxis(tile, axis, 0), me), 0, axis)

    def unrotate(tile, axis):
        back = lax.rem(groups - me, groups)
        return jnp.moveaxis(rolled(jnp.moveaxis(tile, axis, 0), back), 0, axis)

    order = (me - jnp.arange(groups, dtype=jnp.int32)) % groups
    columns = (order[:, None] * local_mom + jnp.arange(local_mom, dtype=jnp.int32)).reshape(-1)
    tables = (jnp.take(cosine_table, columns, axis=1), jnp.take(sine_table, columns, axis=1))

    def shifted(value, by):
        if by % groups == 0:
            return value
        return lax.ppermute(value, "mom", [(i, (i + by) % groups) for i in range(groups)])

    def to_sites(chunk):
        return [
            shifted(chunk[:, :, s * piece_rows : (s + 1) * piece_rows], s) for s in range(groups)
        ]

    def to_momentum(pieces):
        return jnp.concatenate([shifted(p, -s) for s, p in enumerate(pieces)], axis=2)

    inward = [(j, j + 1) for j in range(half - 1)] + [(j, j - 1) for j in range(half + 1, line)]
    across = [(half - 1, half), (half, half - 1)]
    low = place < half
    distance = jnp.where(low, half - 1 - place, place - half)

    def move(value, pairs):
        return lax.ppermute(value, "trow", pairs)

    def near_tiles(tile):
        tiles = [tile]
        for _ in range(half - 1):
            tiles.append(move(tiles[-1], inward))
        return tiles

    def outward(tiles):
        result = tiles[0]
        for d in range(1, half):
            moving = tiles[d]
            for step in range(1, d + 1):
                pairs = [(half - step, half - 1 - step), (half - 1 + step, half + step)]
                moving = move(moving, pairs)
            result = jnp.where(distance == d, moving, result)
        return result

    free = rotate(g_free, 2)
    greater = rotate(g_greater_t, 2)

    def chunk_of(tile, axis, c):
        return lax.slice_in_dim(tile, c * chunk_rows, (c + 1) * chunk_rows, axis=axis)

    piece = (2, local_mom, piece_rows, tile_cols)
    state = {}

    def gate():
        names = sorted(state)
        held = lax.optimization_barrier(tuple(state[n] for n in names))
        state.update(zip(names, held))

    def stage_spread(sweep, c):
        if sweep == 0:
            both = jnp.concatenate([chunk_of(free, 2, c), chunk_of(greater, 2, c)], axis=0)
            state["near", 0, c] = near_tiles(chunk_of(free, 2, c))
        else:
            both = state.pop(("green", sweep, c))
        state["sites", sweep, c] = to_sites(both)

    def stage_sites(sweep, c):
        arrived = state.pop(("sites", sweep, c))
        if sweep == 0:
            state["mirror", 0, c] = call_local(
                functools.partial(mirror_kernel, groups, local_mom),
                tables,
                [a[2:] for a in arrived],
                [(2, momenta, piece_rows, tile_cols)],
            )[0]
            arrived = [a[:2] for a in arrived]
        pieces = call_local(
            functools.partial(sigma_kernel, groups, local_mom),
            tables,
            arrived + [state["mirror", 0, c]],
            [piece] * groups,
        )
        state["sigma", sweep, c] = to_momentum(pieces)

    def stage_line(sweep, c):
        near = near_tiles(state.pop(("sigma", sweep, c)))
        state["nearby", sweep, c] = near
        state["far", sweep, c] = [move(near[0], across)]

    def stage_across(sweep, c):
        near = state["nearby", sweep, c]
        state["far", sweep, c] = state["far", sweep, c] + [move(t, across) for t in near[1:]]

    def stage_product(sweep, c):
        near = state.pop(("nearby", sweep, c))
        far = state.pop(("far", sweep, c))
        blocks = [jnp.where(low, a, b) for a, b in zip(near[::-1] + far, far[::-1] + near)]
        joined = jnp.concatenate(blocks, axis=3) * weights
        product = jnp.einsum(
            "krs,ksc->krc",
            jnp.concatenate([joined[0], joined[1]], axis=1),
            right_side(sweep),
            precision=lax.Precision.HIGH,
            preferred_element_type=jnp.float32,
        )
        top, bottom = product[:, :chunk_rows], product[:, chunk_rows:]
        real = top[:, :, :part_cols] - bottom[:, :, part_cols:]
        imag = top[:, :, part_cols:] + bottom[:, :, :part_cols]
        state["hub", sweep, c] = hub_chunk(c) + jnp.concatenate([real, imag], axis=2)

    def stage_out(sweep, c):
        hub = state["hub", sweep, c]
        tiles = [
            jnp.stack(
                [
                    lax.slice_in_dim(hub, col, col + tile_cols, axis=2)
                    for col in (d * tile_cols, part_cols + d * tile_cols)
                ]
            )
            for d in range(half)
        ]
        state["green", sweep + 1, c] = outward(tiles)

    def hub_chunk(c):
        near = state["near", 0, c]
        return jnp.concatenate([t[0] for t in near] + [t[1] for t in near], axis=2)

    def right_side(sweep):
        if ("right", sweep) not in state:
            parts = [
                hub_chunk(c) if sweep == 0 else state.pop(("hub", sweep - 1, c))
                for c in range(chunks)
            ]
            whole = unrotate(jnp.concatenate(parts, axis=1), 1)
            state["right", sweep] = lax.all_gather(whole, "tcol", axis=1, tiled=True)
        return state["right", sweep]

    stages = [stage_spread, stage_sites, stage_line, stage_across, stage_product, stage_out]
    depth = len(stages)
    gap = max(chunks, depth)
    for tick in range((ITERS - 1) * gap + chunks + depth - 1):
        for late in reversed(range(depth)):
            for sweep in range(ITERS):
                c = tick - late - sweep * gap
                if 0 <= c < chunks:
                    stages[late](sweep, c)
        gate()
    return unrotate(
        jnp.concatenate([state["green", ITERS, c] for c in range(chunks)], axis=2), 2
    )


def solution(mesh):
    placed = (P(None, "mom", "tcol", "trow"), P(None, "mom", "tcol", "trow"), P(), P())
    return jax.shard_map(
        body, mesh=mesh, in_specs=placed, out_specs=P(None, "mom", "tcol", "trow"), check_vma=False
    )
```

```python
import functools
import math

import jax
import jax.numpy as jnp
from jax import lax
from jax.experimental import pallas as pl
from jax.experimental.pallas import tpu as pltpu
from jax.sharding import PartitionSpec as P

LY = 4
ITERS = 2
CHUNKS = 4
SUBLANES = 8


def phase_tables(momentum_map):
    momenta = momentum_map.shape[0]
    across = momenta // LY
    site_index = jnp.arange(momenta, dtype=jnp.int32)
    wave_x = momentum_map % across
    wave_y = momentum_map // across
    site_x = site_index % across
    site_y = site_index // across
    phase_turns = (
        site_x[:, None] * wave_x[None, :] % across * LY
        + site_y[:, None] * wave_y[None, :] % LY * across
    )
    angles = phase_turns.astype(jnp.float32) * (2.0 * math.pi / momenta)
    norm_scale = 1.0 / math.sqrt(momenta)
    return (jnp.cos(angles) * norm_scale, jnp.sin(angles) * norm_scale)


def over_sites(momenta, one_site):
    if momenta <= 8:
        for site in range(momenta):
            one_site(site, site == 0)
    else:
        one_site(0, True)
        pl.loop(1, momenta)(lambda site: one_site(site, False))


def transform(cos_ref, sin_ref, site, reals, imags, sign):
    total_real = total_imag = None
    for k, (real, imag) in enumerate(zip(reals, imags)):
        c = cos_ref[site, k]
        s = sin_ref[site, k]
        if sign < 0:
            term_real, term_imag = c * real + s * imag, c * imag - s * real
        else:
            term_real, term_imag = c * real - s * imag, c * imag + s * real
        total_real = term_real if k == 0 else total_real + term_real
        total_imag = term_imag if k == 0 else total_imag + term_imag
    return total_real, total_imag


def momentum_values(refs, local_mom, rows):
    reals = [ref[0, j, rows, :] for ref in refs for j in range(local_mom)]
    imags = [ref[1, j, rows, :] for ref in refs for j in range(local_mom)]
    return reals, imags


def mirror_kernel(groups, local_mom, *refs):
    cos_ref, sin_ref = refs[:2]
    ins = refs[2 : 2 + groups]
    out = refs[2 + groups]
    height = out.shape[2]

    @pl.loop(0, height // SUBLANES)
    def _(step):
        rows = pl.ds(pl.multiple_of(step * SUBLANES, SUBLANES), SUBLANES)
        reals, imags = momentum_values(ins, local_mom, rows)

        def one_site(site, first):
            real, imag = transform(cos_ref, sin_ref, site, reals, imags, -1)
            out[0, site, rows, :] = real
            out[1, site, rows, :] = imag

        over_sites(groups * local_mom, one_site)


def sigma_kernel(groups, local_mom, *refs):
    cos_ref, sin_ref = refs[:2]
    ins = refs[2 : 2 + groups]
    mirror = refs[2 + groups]
    outs = refs[3 + groups :]
    height = mirror.shape[2]
    momenta = groups * local_mom

    @pl.loop(0, height // SUBLANES)
    def _(step):
        rows = pl.ds(pl.multiple_of(step * SUBLANES, SUBLANES), SUBLANES)
        reals, imags = momentum_values(ins, local_mom, rows)
        held = {}

        def one_site(site, first):
            a, b = transform(cos_ref, sin_ref, site, reals, imags, 1)
            square_real = a * a - b * b
            square_imag = 2.0 * a * b
            m_real = mirror[0, site, rows, :]
            m_imag = mirror[1, site, rows, :]
            source_real = square_real * m_real - square_imag * m_imag
            source_imag = square_real * m_imag + square_imag * m_real
            for k in range(momenta):
                c = cos_ref[site, k]
                s = sin_ref[site, k]
                term = (c * source_real + s * source_imag, c * source_imag - s * source_real)
                if momenta <= 8:
                    held[k] = term if first else (held[k][0] + term[0], held[k][1] + term[1])
                else:
                    ref, j = outs[k // local_mom], k % local_mom
                    for part in range(2):
                        before = 0.0 if first else ref[part, j, rows, :]
                        ref[part, j, rows, :] = before + term[part]

        over_sites(momenta, one_site)
        for k, term in held.items():
            ref, j = outs[k // local_mom], k % local_mom
            ref[0, j, rows, :] = term[0]
            ref[1, j, rows, :] = term[1]


def call_local(kernel, tables, operands, shapes):
    smem = pl.BlockSpec(memory_space=pltpu.SMEM)
    vmem = pl.BlockSpec(memory_space=pltpu.VMEM)
    cells = math.prod(operands[0].shape) * len(operands)
    return pl.pallas_call(
        kernel,
        out_shape=[jax.ShapeDtypeStruct(s, jnp.float32) for s in shapes],
        in_specs=[smem, smem] + [vmem] * len(operands),
        out_specs=[vmem] * len(shapes),
        compiler_params=pltpu.CompilerParams(vmem_limit_bytes=32 * 2**20),
        cost_estimate=pl.CostEstimate(flops=40 * cells, bytes_accessed=12 * cells, transcendentals=0),
    )(*tables, *operands)


def body(g_free, g_greater_t, momentum_map, weights):
    cosine_table, sine_table = phase_tables(momentum_map)
    groups = lax.axis_size("mom")
    me = lax.axis_index("mom")
    line = lax.axis_size("trow")
    place = lax.axis_index("trow")
    _, local_mom, tile_rows, tile_cols = g_free.shape
    momenta = groups * local_mom
    half = line // 2
    chunks = CHUNKS
    while tile_rows % (chunks * groups * SUBLANES):
        chunks -= 1
    piece_rows = tile_rows // (chunks * groups)
    chunk_rows = piece_rows * groups
    part_cols = half * tile_cols

    def rolled(rows_first, start):
        shape = rows_first.shape
        cut = rows_first.reshape((chunks, groups, piece_rows) + shape[1:])
        twice = jnp.concatenate([cut, cut], axis=1)
        return lax.dynamic_slice_in_dim(twice, start, groups, 1).reshape(shape)

    def rotate(tile, axis):
        return jnp.moveaxis(rolled(jnp.moveaxis(tile, axis, 0), me), 0, axis)

    def unrotate(tile, axis):
        back = lax.rem(groups - me, groups)
        return jnp.moveaxis(rolled(jnp.moveaxis(tile, axis, 0), back), 0, axis)

    order = (me - jnp.arange(groups, dtype=jnp.int32)) % groups
    columns = (order[:, None] * local_mom + jnp.arange(local_mom, dtype=jnp.int32)).reshape(-1)
    tables = (jnp.take(cosine_table, columns, axis=1), jnp.take(sine_table, columns, axis=1))

    def shifted(value, by):
        if by % groups == 0:
            return value
        return lax.ppermute(value, "mom", [(i, (i + by) % groups) for i in range(groups)])

    def to_sites(chunk):
        return [
            shifted(chunk[:, :, s * piece_rows : (s + 1) * piece_rows], s) for s in range(groups)
        ]

    def to_momentum(pieces):
        return jnp.concatenate([shifted(p, -s) for s, p in enumerate(pieces)], axis=2)

    low = place < half
    distance = jnp.where(low, half - 1 - place, place - half)

    def near_tile(tile, d):
        if d == 0:
            return tile
        return lax.ppermute(tile, "trow", [(half - 1 - d, half - 1), (half + d, half)])

    def far_tile(tile, d):
        return lax.ppermute(tile, "trow", [(half - 1 - d, half), (half + d, half - 1)])

    def outward(tiles):
        result = tiles[0]
        for d in range(1, half):
            pairs = [(half - 1, half - 1 - d), (half, half + d)]
            result = jnp.where(distance == d, lax.ppermute(tiles[d], "trow", pairs), result)
        return result

    free = rotate(g_free, 2)
    greater = rotate(g_greater_t, 2)

    def chunk_of(tile, axis, c):
        return lax.slice_in_dim(tile, c * chunk_rows, (c + 1) * chunk_rows, axis=axis)

    piece = (2, local_mom, piece_rows, tile_cols)
    state = {}

    def gate():
        names = sorted(state, key=str)
        held = lax.optimization_barrier(tuple(state[n] for n in names))
        state.update(zip(names, held))

    near_free = [near_tile(g_free, d) for d in range(half)]

    def hub_tiles(near):
        return jnp.concatenate([t[0] for t in near] + [t[1] for t in near], axis=2)

    def stage_sites(sweep, c):
        if sweep == 0:
            both = jnp.concatenate([chunk_of(free, 2, c), chunk_of(greater, 2, c)], axis=0)
        else:
            both = state.pop(("green", sweep, c))
        arrived = to_sites(both)
        if sweep == 0:
            state["mirror", 0, c] = call_local(
                functools.partial(mirror_kernel, groups, local_mom),
                tables,
                [a[2:] for a in arrived],
                [(2, momenta, piece_rows, tile_cols)],
            )[0]
            arrived = [a[:2] for a in arrived]
        pieces = call_local(
            functools.partial(sigma_kernel, groups, local_mom),
            tables,
            arrived + [state["mirror", 0, c]],
            [piece] * groups,
        )
        state["sigma", sweep, c] = to_momentum(pieces)

    def stage_line(sweep, c):
        sigma = state.pop(("sigma", sweep, c))
        state["near", sweep, c] = [near_tile(sigma, d) for d in range(half)]
        state["far", sweep, c] = [far_tile(sigma, d) for d in range(half)]

    def stage_product(sweep, c):
        near = state.pop(("near", sweep, c))
        far = state.pop(("far", sweep, c))
        blocks = [jnp.where(low, a, b) for a, b in zip(near[::-1] + far, far[::-1] + near)]
        shared = right_side(sweep)
        joined = jnp.concatenate(blocks, axis=3) * weights
        product = jnp.einsum(
            "krs,ksc->krc",
            jnp.concatenate([joined[0], joined[1]], axis=1),
            shared,
            precision=lax.Precision.HIGH,
            preferred_element_type=jnp.float32,
        )
        top, bottom = product[:, :chunk_rows], product[:, chunk_rows:]
        real = top[:, :, :part_cols] - bottom[:, :, part_cols:]
        imag = top[:, :, part_cols:] + bottom[:, :, :part_cols]
        hub = chunk_of(state["hub_free"], 1, c) + jnp.concatenate([real, imag], axis=2)
        state["hub", sweep, c] = hub
        tiles = [
            jnp.stack(
                [
                    lax.slice_in_dim(hub, col, col + tile_cols, axis=2)
                    for col in (d * tile_cols, part_cols + d * tile_cols)
                ]
            )
            for d in range(half)
        ]
        state["green", sweep + 1, c] = outward(tiles)

    def right_side(sweep):
        if ("right", sweep) not in state:
            if sweep == 0:
                whole = hub_tiles(state.pop("near_free"))
                state["hub_free"] = rotate(whole, 1)
            else:
                parts = [state.pop(("hub", sweep - 1, c)) for c in range(chunks)]
                whole = unrotate(jnp.concatenate(parts, axis=1), 1)
            state["right", sweep] = lax.all_gather(whole, "tcol", axis=1, tiled=True)
        return state["right", sweep]

    stages = [stage_sites, stage_line, stage_product]
    depth = len(stages)
    gap = max(chunks, depth)
    for tick in range((ITERS - 1) * gap + chunks + depth - 1):
        for late in reversed(range(depth)):
            for sweep in range(ITERS):
                c = tick - late - sweep * gap
                if 0 <= c < chunks:
                    stages[late](sweep, c)
        if tick == depth - 2:
            state["near_free"] = near_free
        gate()
    return unrotate(
        jnp.concatenate([state["green", ITERS, c] for c in range(chunks)], axis=2), 2
    )


def solution(mesh):
    placed = (P(None, "mom", "tcol", "trow"), P(None, "mom", "tcol", "trow"), P(), P())
    return jax.shard_map(
        body, mesh=mesh, in_specs=placed, out_specs=P(None, "mom", "tcol", "trow"), check_vma=False
    )
```

```python
import functools
import math

import jax
import jax.numpy as jnp
from jax import lax
from jax.experimental import pallas as pl
from jax.experimental.pallas import tpu as pltpu
from jax.sharding import PartitionSpec as P

LY = 4
ITERS = 2
CHUNKS = 4
SUBLANES = 8


def phase_tables(momentum_map):
    momenta = momentum_map.shape[0]
    across = momenta // LY
    site_index = jnp.arange(momenta, dtype=jnp.int32)
    wave_x = momentum_map % across
    wave_y = momentum_map // across
    site_x = site_index % across
    site_y = site_index // across
    phase_turns = (
        site_x[:, None] * wave_x[None, :] % across * LY
        + site_y[:, None] * wave_y[None, :] % LY * across
    )
    angles = phase_turns.astype(jnp.float32) * (2.0 * math.pi / momenta)
    norm_scale = 1.0 / math.sqrt(momenta)
    return (jnp.cos(angles) * norm_scale, jnp.sin(angles) * norm_scale)


def over_sites(momenta, one_site):
    if momenta <= 8:
        for site in range(momenta):
            one_site(site, site == 0)
    else:
        one_site(0, True)
        pl.loop(1, momenta)(lambda site: one_site(site, False))


def transform(cos_ref, sin_ref, site, reals, imags, sign):
    total_real = total_imag = None
    for k, (real, imag) in enumerate(zip(reals, imags)):
        c = cos_ref[site, k]
        s = sin_ref[site, k]
        if sign < 0:
            term_real, term_imag = c * real + s * imag, c * imag - s * real
        else:
            term_real, term_imag = c * real - s * imag, c * imag + s * real
        total_real = term_real if k == 0 else total_real + term_real
        total_imag = term_imag if k == 0 else total_imag + term_imag
    return total_real, total_imag


def momentum_values(refs, local_mom, rows):
    reals = [ref[0, j, rows, :] for ref in refs for j in range(local_mom)]
    imags = [ref[1, j, rows, :] for ref in refs for j in range(local_mom)]
    return reals, imags


def mirror_kernel(groups, local_mom, *refs):
    cos_ref, sin_ref = refs[:2]
    ins = refs[2 : 2 + groups]
    out = refs[2 + groups]
    height = out.shape[2]

    @pl.loop(0, height // SUBLANES)
    def _(step):
        rows = pl.ds(pl.multiple_of(step * SUBLANES, SUBLANES), SUBLANES)
        reals, imags = momentum_values(ins, local_mom, rows)

        def one_site(site, first):
            real, imag = transform(cos_ref, sin_ref, site, reals, imags, -1)
            out[0, site, rows, :] = real
            out[1, site, rows, :] = imag

        over_sites(groups * local_mom, one_site)


def sigma_kernel(groups, local_mom, *refs):
    cos_ref, sin_ref = refs[:2]
    ins = refs[2 : 2 + groups]
    mirror = refs[2 + groups]
    outs = refs[3 + groups :]
    height = mirror.shape[2]
    momenta = groups * local_mom

    @pl.loop(0, height // SUBLANES)
    def _(step):
        rows = pl.ds(pl.multiple_of(step * SUBLANES, SUBLANES), SUBLANES)
        reals, imags = momentum_values(ins, local_mom, rows)
        held = {}

        def one_site(site, first):
            a, b = transform(cos_ref, sin_ref, site, reals, imags, 1)
            square_real = a * a - b * b
            square_imag = 2.0 * a * b
            m_real = mirror[0, site, rows, :]
            m_imag = mirror[1, site, rows, :]
            source_real = square_real * m_real - square_imag * m_imag
            source_imag = square_real * m_imag + square_imag * m_real
            for k in range(momenta):
                c = cos_ref[site, k]
                s = sin_ref[site, k]
                term = (c * source_real + s * source_imag, c * source_imag - s * source_real)
                if momenta <= 8:
                    held[k] = term if first else (held[k][0] + term[0], held[k][1] + term[1])
                else:
                    ref, j = outs[k // local_mom], k % local_mom
                    for part in range(2):
                        before = 0.0 if first else ref[part, j, rows, :]
                        ref[part, j, rows, :] = before + term[part]

        over_sites(momenta, one_site)
        for k, term in held.items():
            ref, j = outs[k // local_mom], k % local_mom
            ref[0, j, rows, :] = term[0]
            ref[1, j, rows, :] = term[1]


def call_local(kernel, tables, operands, shapes):
    smem = pl.BlockSpec(memory_space=pltpu.SMEM)
    vmem = pl.BlockSpec(memory_space=pltpu.VMEM)
    return pl.pallas_call(
        kernel,
        out_shape=[jax.ShapeDtypeStruct(s, jnp.float32) for s in shapes],
        in_specs=[smem, smem] + [vmem] * len(operands),
        out_specs=[vmem] * len(shapes),
        compiler_params=pltpu.CompilerParams(vmem_limit_bytes=32 * 2**20),
        cost_estimate=pl.CostEstimate(flops=1, bytes_accessed=1, transcendentals=0),
    )(*tables, *operands)


def halves(value):
    high = value.astype(jnp.bfloat16)
    return high, (value - high.astype(jnp.float32)).astype(jnp.bfloat16)


def product_kernel(line, spot_ref, *refs):
    tiles = refs[:line]
    high_ref, low_ref, free_ref, out_ref, left_high, left_low = refs[line:]
    _, local_mom, rows, cols = tiles[0].shape

    @pl.when(pl.program_id(0) == 0)
    def _():
        for t, tile in enumerate(tiles):
            lanes = pl.ds(pl.multiple_of(spot_ref[t] * cols, 128), cols)
            for j in range(local_mom):
                for part in range(2):
                    high, low = halves(tile[part, j])
                    left_high[j, part * rows : (part + 1) * rows, lanes] = high
                    left_low[j, part * rows : (part + 1) * rows, lanes] = low

    for j in range(local_mom):
        right = high_ref[0, j]
        dot = functools.partial(jnp.dot, preferred_element_type=jnp.float32)
        total = dot(left_low[j], right) + dot(left_high[j], low_ref[0, j])
        total = total + dot(left_high[j], right)
        top, bottom = total[:rows], total[rows:]
        out_ref[0, 0, j] = free_ref[0, 0, j] + (top[:, :cols] - bottom[:, cols:])
        out_ref[0, 1, j] = free_ref[0, 1, j] + (top[:, cols:] + bottom[:, :cols])


def product(spots, tiles, right, free, chunk):
    high, low = right
    half, _, local_mom, _, cols = free.shape
    rows = tiles[0].shape[2]
    line = len(tiles)
    depth = high.shape[2]
    whole = pl.BlockSpec(memory_space=pltpu.VMEM)
    right_spec = pl.BlockSpec((1, local_mom, depth, 2 * cols), lambda d: (d, 0, 0, 0))
    return pl.pallas_call(
        functools.partial(product_kernel, line),
        grid=(half,),
        out_shape=jax.ShapeDtypeStruct((half, 2, local_mom, rows, cols), jnp.float32),
        in_specs=[pl.BlockSpec(memory_space=pltpu.SMEM)]
        + [whole] * line
        + [
            right_spec,
            right_spec,
            pl.BlockSpec((1, 2, local_mom, rows, cols), lambda d: (d, 0, 0, chunk, 0)),
        ],
        out_specs=pl.BlockSpec((1, 2, local_mom, rows, cols), lambda d: (d, 0, 0, 0, 0)),
        scratch_shapes=[pltpu.VMEM((local_mom, 2 * rows, depth), jnp.bfloat16)] * 2,
        compiler_params=pltpu.CompilerParams(vmem_limit_bytes=40 * 2**20),
        cost_estimate=pl.CostEstimate(flops=1, bytes_accessed=1, transcendentals=0),
    )(spots, *tiles, high, low, free)


def body(g_free, g_greater_t, momentum_map, weights):
    cosine_table, sine_table = phase_tables(momentum_map)
    groups = lax.axis_size("mom")
    me = lax.axis_index("mom")
    line = lax.axis_size("trow")
    place = lax.axis_index("trow")
    _, local_mom, tile_rows, tile_cols = g_free.shape
    momenta = groups * local_mom
    half = line // 2
    chunks = CHUNKS
    while tile_rows % (chunks * groups * SUBLANES):
        chunks -= 1
    piece_rows = tile_rows // (chunks * groups)
    chunk_rows = piece_rows * groups

    def rolled(rows_first, start):
        shape = rows_first.shape
        cut = rows_first.reshape((chunks, groups, piece_rows) + shape[1:])
        twice = jnp.concatenate([cut, cut], axis=1)
        return lax.dynamic_slice_in_dim(twice, start, groups, 1).reshape(shape)

    def rotate(tile, axis):
        return jnp.moveaxis(rolled(jnp.moveaxis(tile, axis, 0), me), 0, axis)

    def unrotate(tile, axis):
        back = lax.rem(groups - me, groups)
        return jnp.moveaxis(rolled(jnp.moveaxis(tile, axis, 0), back), 0, axis)

    order = (me - jnp.arange(groups, dtype=jnp.int32)) % groups
    columns = (order[:, None] * local_mom + jnp.arange(local_mom, dtype=jnp.int32)).reshape(-1)
    tables = (jnp.take(cosine_table, columns, axis=1), jnp.take(sine_table, columns, axis=1))

    def shifted(value, by):
        if by % groups == 0:
            return value
        return lax.ppermute(value, "mom", [(i, (i + by) % groups) for i in range(groups)])

    def to_sites(chunk):
        return [
            shifted(chunk[:, :, s * piece_rows : (s + 1) * piece_rows], s) for s in range(groups)
        ]

    def to_momentum(pieces):
        return jnp.concatenate([shifted(p, -s) for s, p in enumerate(pieces)], axis=2)

    low = place < half
    distance = jnp.where(low, half - 1 - place, place - half)

    def near_tile(tile, d):
        if d == 0:
            return tile
        return lax.ppermute(tile, "trow", [(half - 1 - d, half - 1), (half + d, half)])

    def far_tile(tile, d):
        return lax.ppermute(tile, "trow", [(half - 1 - d, half), (half + d, half - 1)])

    def outward(tiles):
        result = tiles[0]
        for d in range(1, half):
            pairs = [(half - 1, half - 1 - d), (half, half + d)]
            result = jnp.where(distance == d, lax.ppermute(tiles[d], "trow", pairs), result)
        return result

    free = rotate(g_free, 2)
    greater = rotate(g_greater_t, 2)

    def chunk_of(tile, axis, c):
        return lax.slice_in_dim(tile, c * chunk_rows, (c + 1) * chunk_rows, axis=axis)

    piece = (2, local_mom, piece_rows, tile_cols)
    state = {}

    def gate():
        names = sorted(state, key=str)
        held = lax.optimization_barrier(tuple(state[n] for n in names))
        state.update(zip(names, held))

    near_free = [near_tile(g_free, d) for d in range(half)]

    def start_sites(sweep, c):
        if sweep == 0:
            both = jnp.concatenate([chunk_of(free, 2, c), chunk_of(greater, 2, c)], axis=0)
        else:
            both = state.pop(("green", sweep, c))
        state["sites", sweep, c] = to_sites(both)

    def end_sites(sweep, c):
        arrived = state.pop(("sites", sweep, c))
        if sweep == 0:
            state["mirror", 0, c] = call_local(
                functools.partial(mirror_kernel, groups, local_mom),
                tables,
                [a[2:] for a in arrived],
                [(2, momenta, piece_rows, tile_cols)],
            )[0]
            arrived = [a[:2] for a in arrived]
        pieces = call_local(
            functools.partial(sigma_kernel, groups, local_mom),
            tables,
            arrived + [state["mirror", 0, c]],
            [piece] * groups,
        )
        state["sigma", sweep, c] = to_momentum(pieces)

    def start_line(sweep, c):
        sigma = state["sigma", sweep, c]
        state["far", sweep, c] = [far_tile(sigma, d) for d in range(1, half)]

    def end_line(sweep, c):
        sigma = state.pop(("sigma", sweep, c))
        state["near", sweep, c] = [near_tile(sigma, d) for d in range(half)]
        state["far", sweep, c] = [far_tile(sigma, 0)] + state["far", sweep, c]

    near_spots = [jnp.where(low, half - 1 - d, half + d) for d in range(half)]
    far_spots = [jnp.where(low, half + d, half - 1 - d) for d in range(half)]
    spots = jnp.stack(near_spots + far_spots).astype(jnp.int32)

    def start_product(sweep, c):
        right = right_side(sweep)
        tiles = state.pop(("near", sweep, c)) + state.pop(("far", sweep, c))
        hub = product(spots, tiles, right, state["hub_free"], c)
        state["hub", sweep, c] = hub

    def end_product(sweep, c):
        hub = state["hub", sweep, c]
        state["green", sweep + 1, c] = outward([hub[d] for d in range(half)])

    def right_side(sweep):
        if ("right", sweep) not in state:
            if sweep == 0:
                plain = jnp.stack(state.pop("near_free"))
                state["hub_free"] = rotate(plain, 3)
            else:
                parts = [state.pop(("hub", sweep - 1, c)) for c in range(chunks)]
                plain = unrotate(jnp.concatenate(parts, axis=3), 3)
            joined = jnp.concatenate([plain[:, 0], plain[:, 1]], axis=3)
            full = lax.all_gather(joined, "tcol", axis=2, tiled=True) * weights[:, None]
            rounded = lax.reduce_precision(full, exponent_bits=8, mantissa_bits=7)
            state["right", sweep] = (
                rounded.astype(jnp.bfloat16),
                (full - rounded).astype(jnp.bfloat16),
            )
        return state["right", sweep]

    stages = [(start_sites, end_sites), (start_line, end_line), (start_product, end_product)]
    depth = len(stages)
    gap = max(chunks, depth)
    for tick in range((ITERS - 1) * gap + chunks + depth - 1):
        for phase in range(2):
            if phase:
                gate()
            for late in reversed(range(depth)):
                for sweep in range(ITERS):
                    c = tick - late - sweep * gap
                    if 0 <= c < chunks:
                        stages[late][phase](sweep, c)
        if tick == depth - 2:
            state["near_free"] = near_free
        gate()
    return unrotate(
        jnp.concatenate([state["green", ITERS, c] for c in range(chunks)], axis=2), 2
    )


def solution(mesh):
    placed = (P(None, "mom", "tcol", "trow"), P(None, "mom", "tcol", "trow"), P(), P())
    return jax.shard_map(
        body, mesh=mesh, in_specs=placed, out_specs=P(None, "mom", "tcol", "trow"), check_vma=False
    )
```

```python
import functools
import math

import jax
import jax.numpy as jnp
from jax import lax
from jax.experimental import pallas as pl
from jax.experimental.pallas import tpu as pltpu
from jax.sharding import PartitionSpec as P

LY = 4
ITERS = 2
CHUNKS = 4
SUBLANES = 8


def phase_tables(momentum_map):
    momenta = momentum_map.shape[0]
    across = momenta // LY
    site_index = jnp.arange(momenta, dtype=jnp.int32)
    wave_x = momentum_map % across
    wave_y = momentum_map // across
    site_x = site_index % across
    site_y = site_index // across
    phase_turns = (
        site_x[:, None] * wave_x[None, :] % across * LY
        + site_y[:, None] * wave_y[None, :] % LY * across
    )
    angles = phase_turns.astype(jnp.float32) * (2.0 * math.pi / momenta)
    norm_scale = 1.0 / math.sqrt(momenta)
    return (jnp.cos(angles) * norm_scale, jnp.sin(angles) * norm_scale)


def over_sites(momenta, one_site):
    if momenta <= 8:
        for site in range(momenta):
            one_site(site, site == 0)
    else:
        one_site(0, True)
        pl.loop(1, momenta)(lambda site: one_site(site, False))


def transform(cos_ref, sin_ref, site, reals, imags, sign):
    total_real = total_imag = None
    for k, (real, imag) in enumerate(zip(reals, imags)):
        c = cos_ref[site, k]
        s = sin_ref[site, k]
        if sign < 0:
            term_real, term_imag = c * real + s * imag, c * imag - s * real
        else:
            term_real, term_imag = c * real - s * imag, c * imag + s * real
        total_real = term_real if k == 0 else total_real + term_real
        total_imag = term_imag if k == 0 else total_imag + term_imag
    return total_real, total_imag


def momentum_values(refs, local_mom, rows):
    reals = [ref[0, j, rows, :] for ref in refs for j in range(local_mom)]
    imags = [ref[1, j, rows, :] for ref in refs for j in range(local_mom)]
    return reals, imags


def mirror_kernel(groups, local_mom, *refs):
    cos_ref, sin_ref = refs[:2]
    ins = refs[2 : 2 + groups]
    out = refs[2 + groups]
    height = out.shape[2]

    @pl.loop(0, height // SUBLANES)
    def _(step):
        rows = pl.ds(pl.multiple_of(step * SUBLANES, SUBLANES), SUBLANES)
        reals, imags = momentum_values(ins, local_mom, rows)

        def one_site(site, first):
            real, imag = transform(cos_ref, sin_ref, site, reals, imags, -1)
            out[0, site, rows, :] = real
            out[1, site, rows, :] = imag

        over_sites(groups * local_mom, one_site)


def sigma_kernel(groups, local_mom, *refs):
    cos_ref, sin_ref = refs[:2]
    ins = refs[2 : 2 + groups]
    mirror = refs[2 + groups]
    outs = refs[3 + groups :]
    height = mirror.shape[2]
    momenta = groups * local_mom

    @pl.loop(0, height // SUBLANES)
    def _(step):
        rows = pl.ds(pl.multiple_of(step * SUBLANES, SUBLANES), SUBLANES)
        reals, imags = momentum_values(ins, local_mom, rows)
        held = {}

        def one_site(site, first):
            a, b = transform(cos_ref, sin_ref, site, reals, imags, 1)
            square_real = a * a - b * b
            square_imag = 2.0 * a * b
            m_real = mirror[0, site, rows, :]
            m_imag = mirror[1, site, rows, :]
            source_real = square_real * m_real - square_imag * m_imag
            source_imag = square_real * m_imag + square_imag * m_real
            for k in range(momenta):
                c = cos_ref[site, k]
                s = sin_ref[site, k]
                term = (c * source_real + s * source_imag, c * source_imag - s * source_real)
                if momenta <= 8:
                    held[k] = term if first else (held[k][0] + term[0], held[k][1] + term[1])
                else:
                    ref, j = outs[k // local_mom], k % local_mom
                    for part in range(2):
                        before = 0.0 if first else ref[part, j, rows, :]
                        ref[part, j, rows, :] = before + term[part]

        over_sites(momenta, one_site)
        for k, term in held.items():
            ref, j = outs[k // local_mom], k % local_mom
            ref[0, j, rows, :] = term[0]
            ref[1, j, rows, :] = term[1]


def call_local(kernel, tables, operands, shapes):
    smem = pl.BlockSpec(memory_space=pltpu.SMEM)
    vmem = pl.BlockSpec(memory_space=pltpu.VMEM)
    return pl.pallas_call(
        kernel,
        out_shape=[jax.ShapeDtypeStruct(s, jnp.float32) for s in shapes],
        in_specs=[smem, smem] + [vmem] * len(operands),
        out_specs=[vmem] * len(shapes),
        compiler_params=pltpu.CompilerParams(vmem_limit_bytes=32 * 2**20),
        cost_estimate=pl.CostEstimate(flops=1, bytes_accessed=1, transcendentals=0),
    )(*tables, *operands)


def halves(value):
    high = value.astype(jnp.bfloat16)
    return high, (value - high.astype(jnp.float32)).astype(jnp.bfloat16)


def product_kernel(line, spot_ref, *refs):
    tiles = refs[:line]
    high_ref, low_ref, free_ref, out_ref, left_high, left_low = refs[line:]
    _, local_mom, rows, cols = tiles[0].shape

    @pl.when(pl.program_id(0) == 0)
    def _():
        for t, tile in enumerate(tiles):
            lanes = pl.ds(pl.multiple_of(spot_ref[t] * cols, 128), cols)
            for j in range(local_mom):
                for part in range(2):
                    high, low = halves(tile[part, j])
                    left_high[j, part * rows : (part + 1) * rows, lanes] = high
                    left_low[j, part * rows : (part + 1) * rows, lanes] = low

    for j in range(local_mom):
        right = high_ref[0, j]
        dot = functools.partial(jnp.dot, preferred_element_type=jnp.float32)
        total = dot(left_low[j], right) + dot(left_high[j], low_ref[0, j])
        total = total + dot(left_high[j], right)
        top, bottom = total[:rows], total[rows:]
        out_ref[0, 0, j] = free_ref[0, 0, j] + (top[:, :cols] - bottom[:, cols:])
        out_ref[0, 1, j] = free_ref[0, 1, j] + (top[:, cols:] + bottom[:, :cols])


def product(spots, tiles, right, free, chunk):
    high, low = right
    half, _, local_mom, _, cols = free.shape
    rows = tiles[0].shape[2]
    line = len(tiles)
    depth = high.shape[2]
    whole = pl.BlockSpec(memory_space=pltpu.VMEM)
    right_spec = pl.BlockSpec((1, local_mom, depth, 2 * cols), lambda d: (d, 0, 0, 0))
    return pl.pallas_call(
        functools.partial(product_kernel, line),
        grid=(half,),
        out_shape=jax.ShapeDtypeStruct((half, 2, local_mom, rows, cols), jnp.float32),
        in_specs=[pl.BlockSpec(memory_space=pltpu.SMEM)]
        + [whole] * line
        + [
            right_spec,
            right_spec,
            pl.BlockSpec((1, 2, local_mom, rows, cols), lambda d: (d, 0, 0, chunk, 0)),
        ],
        out_specs=pl.BlockSpec((1, 2, local_mom, rows, cols), lambda d: (d, 0, 0, 0, 0)),
        scratch_shapes=[pltpu.VMEM((local_mom, 2 * rows, depth), jnp.bfloat16)] * 2,
        compiler_params=pltpu.CompilerParams(vmem_limit_bytes=40 * 2**20),
        cost_estimate=pl.CostEstimate(flops=1, bytes_accessed=1, transcendentals=0),
    )(spots, *tiles, high, low, free)


def body(g_free, g_greater_t, momentum_map, weights):
    cosine_table, sine_table = phase_tables(momentum_map)
    groups = lax.axis_size("mom")
    me = lax.axis_index("mom")
    line = lax.axis_size("trow")
    place = lax.axis_index("trow")
    _, local_mom, tile_rows, tile_cols = g_free.shape
    momenta = groups * local_mom
    half = line // 2
    chunks = CHUNKS
    while tile_rows % (chunks * groups * SUBLANES):
        chunks -= 1
    piece_rows = tile_rows // (chunks * groups)
    chunk_rows = piece_rows * groups

    def rolled(rows_first, start):
        shape = rows_first.shape
        cut = rows_first.reshape((chunks, groups, piece_rows) + shape[1:])
        twice = jnp.concatenate([cut, cut], axis=1)
        return lax.dynamic_slice_in_dim(twice, start, groups, 1).reshape(shape)

    def rotate(tile, axis):
        return jnp.moveaxis(rolled(jnp.moveaxis(tile, axis, 0), me), 0, axis)

    def unrotate(tile, axis):
        back = lax.rem(groups - me, groups)
        return jnp.moveaxis(rolled(jnp.moveaxis(tile, axis, 0), back), 0, axis)

    order = (me - jnp.arange(groups, dtype=jnp.int32)) % groups
    columns = (order[:, None] * local_mom + jnp.arange(local_mom, dtype=jnp.int32)).reshape(-1)
    tables = (jnp.take(cosine_table, columns, axis=1), jnp.take(sine_table, columns, axis=1))

    def shifted(value, by):
        if by % groups == 0:
            return value
        return lax.ppermute(value, "mom", [(i, (i + by) % groups) for i in range(groups)])

    def to_sites(chunk):
        return [
            shifted(chunk[:, :, s * piece_rows : (s + 1) * piece_rows], s) for s in range(groups)
        ]

    def to_momentum(pieces):
        return jnp.concatenate([shifted(p, -s) for s, p in enumerate(pieces)], axis=2)

    low = place < half
    distance = jnp.where(low, half - 1 - place, place - half)

    def near_tile(tile, d):
        if d == 0:
            return tile
        return lax.ppermute(tile, "trow", [(half - 1 - d, half - 1), (half + d, half)])

    def across(tile):
        return lax.ppermute(tile, "trow", [(half - 1, half), (half, half - 1)])

    def outward(tiles):
        result = tiles[0]
        for d in range(1, half):
            pairs = [(half - 1, half - 1 - d), (half, half + d)]
            result = jnp.where(distance == d, lax.ppermute(tiles[d], "trow", pairs), result)
        return result

    free = rotate(g_free, 2)
    greater = rotate(g_greater_t, 2)

    def chunk_of(tile, axis, c):
        return lax.slice_in_dim(tile, c * chunk_rows, (c + 1) * chunk_rows, axis=axis)

    piece = (2, local_mom, piece_rows, tile_cols)
    state = {}

    def gate():
        names = sorted(state, key=str)
        held = lax.optimization_barrier(tuple(state[n] for n in names))
        state.update(zip(names, held))

    near_free = [near_tile(g_free, d) for d in range(half)]

    def start_sites(sweep, c):
        if sweep == 0:
            both = jnp.concatenate([chunk_of(free, 2, c), chunk_of(greater, 2, c)], axis=0)
        else:
            both = state.pop(("green", sweep, c))
        state["sites", sweep, c] = to_sites(both)

    def end_sites(sweep, c):
        arrived = state.pop(("sites", sweep, c))
        if sweep == 0:
            state["mirror", 0, c] = call_local(
                functools.partial(mirror_kernel, groups, local_mom),
                tables,
                [a[2:] for a in arrived],
                [(2, momenta, piece_rows, tile_cols)],
            )[0]
            arrived = [a[:2] for a in arrived]
        pieces = call_local(
            functools.partial(sigma_kernel, groups, local_mom),
            tables,
            arrived + [state["mirror", 0, c]],
            [piece] * groups,
        )
        state["sigma", sweep, c] = to_momentum(pieces)

    def start_line(sweep, c):
        sigma = state.pop(("sigma", sweep, c))
        state["near", sweep, c] = [near_tile(sigma, d) for d in range(half)]
        state["far", sweep, c] = [across(sigma)]

    def end_line(sweep, c):
        near = state["near", sweep, c]
        state["far", sweep, c] = state["far", sweep, c] + [across(t) for t in near[1:]]

    near_spots = [jnp.where(low, half - 1 - d, half + d) for d in range(half)]
    far_spots = [jnp.where(low, half + d, half - 1 - d) for d in range(half)]
    spots = jnp.stack(near_spots + far_spots).astype(jnp.int32)

    def start_product(sweep, c):
        right = right_side(sweep)
        tiles = state.pop(("near", sweep, c)) + state.pop(("far", sweep, c))
        hub = product(spots, tiles, right, state["hub_free"], c)
        state["hub", sweep, c] = hub

    def end_product(sweep, c):
        hub = state["hub", sweep, c]
        state["green", sweep + 1, c] = outward([hub[d] for d in range(half)])

    def right_side(sweep):
        if ("right", sweep) not in state:
            if sweep == 0:
                plain = jnp.stack(state.pop("near_free"))
                state["hub_free"] = rotate(plain, 3)
            else:
                state.pop(("right", sweep - 1))
                parts = [state["hub", sweep - 1, c] for c in range(chunks)]
                plain = unrotate(jnp.concatenate(parts, axis=3), 3)
            joined = jnp.concatenate([plain[:, 0], plain[:, 1]], axis=3)
            full = lax.all_gather(joined, "tcol", axis=2, tiled=True) * weights[:, None]
            rounded = lax.reduce_precision(full, exponent_bits=8, mantissa_bits=7)
            state["right", sweep] = (
                rounded.astype(jnp.bfloat16),
                (full - rounded).astype(jnp.bfloat16),
            )
        return state["right", sweep]

    stages = [start_sites, end_sites, start_line, end_line, start_product, end_product]
    depth = len(stages)
    gap = max(chunks, depth)
    for tick in range((ITERS - 1) * gap + chunks + depth - 1):
        for late in reversed(range(depth)):
            for sweep in range(ITERS):
                c = tick - late - sweep * gap
                if 0 <= c < chunks:
                    stages[late](sweep, c)
        if tick == depth - 4:
            state["near_free"] = near_free
        if tick == depth - 3:
            right_side(0)
        for sweep in range(1, ITERS):
            if tick == (sweep - 1) * gap + chunks + depth - 2:
                right_side(sweep)
        gate()
    return unrotate(
        jnp.concatenate([state["green", ITERS, c] for c in range(chunks)], axis=2), 2
    )


def solution(mesh):
    placed = (P(None, "mom", "tcol", "trow"), P(None, "mom", "tcol", "trow"), P(), P())
    return jax.shard_map(
        body, mesh=mesh, in_specs=placed, out_specs=P(None, "mom", "tcol", "trow"), check_vma=False
    )
```
